256 devices in a mesh: row: 32 (over y, z), col: 8 (over x, core).
Axes of the slice: x: 4, y: 4, z: 8, core: 2. Of those that a mesh axis runs over, the one named last changes fastest.
Arguments:
- embeddings: bfloat16 [4096, 1024], P(('row', 'col')), may hold values from -20 to 20
- group_ids: int32 [4096], P(('row', 'col')), may hold values from 0 to 1023, as said below
Outputs:
- loss: float32 [], replicated
- grad: bfloat16 [4096, 1024], P(('row', 'col'))
The draws below stay inside these ranges and needn't reach their ends.
Inputs may be any that keep to these rules, and one draw needn't show every extreme that they name: `group_ids`: every group id is held by exactly 4 rows, spread over the batch.
All inputs are finite; a program needn't handle non-finite values.
Results may differ from the reference program's by a relative error of at most 0.0045.
Values may be sent and summed in bfloat16 or wider, within the bound.
A program may use at most 64 MiB of HBM per device.

```python
import jax
import jax.numpy as jnp
from jax import lax

D = 1024
GROUP = 4
N = 4096
N_ROW = 32


def draw_embeddings(key, part):
    values = jnp.clip(jax.random.normal(key, (N, D), jnp.float32), -6.0, 6.0)
    signs = jnp.where(jax.random.bernoulli(jax.random.fold_in(key, 11), 0.5, (D,)), 1.0, -1.0).astype(jnp.float32)
    index = jnp.arange(N)
    blocks = index // 64
    within = index % 64
    target = 100.0 + 80.0 * (blocks % 4).astype(jnp.float32) + 1.5 * within.astype(jnp.float32)
    strength = jnp.sqrt(target / jnp.sqrt(jnp.float32(D)))
    aligned = within < 3
    values = jnp.where(aligned[:, None], strength[:, None] * signs[None, :], values)
    return values.astype(jnp.bfloat16)


def draw_group_ids(key, part):
    order = jax.random.permutation(key, N)
    return (order // GROUP).astype(jnp.int32)


def setup_inputs(seed: int = 0) -> dict:
    keys = jax.random.split(jax.random.key(seed), 3)
    embeddings = draw_embeddings(jax.random.fold_in(keys[2], 71), 0)
    group_ids = draw_group_ids(jax.random.fold_in(keys[2], 71), 0)
    return dict(embeddings=embeddings, group_ids=group_ids)


def reference(embeddings, group_ids):
    scale = 1.0 / jnp.sqrt(jnp.float32(D))
    block = N // N_ROW
    starts = jnp.arange(N_ROW, dtype=jnp.int32) * block
    every = jnp.arange(N, dtype=jnp.int32)

    def tile(start):
        queries = lax.dynamic_slice_in_dim(embeddings, start, block, 0)
        query_groups = lax.dynamic_slice_in_dim(group_ids, start, block, 0)
        index = start + jnp.arange(block, dtype=jnp.int32)
        scores = lax.dot_general(queries, embeddings, (((1,), (1,)), ((), ())), preferred_element_type=jnp.float32) * scale
        selfs = index[:, None] == every[None, :]
        positive = jnp.logical_and(query_groups[:, None] == group_ids[None, :], jnp.logical_not(selfs))
        masked = jnp.where(selfs, jnp.float32(-1e+30), scores)
        return (queries, scores, masked, positive)

    def stats(start):
        queries, scores, masked, positive = tile(start)
        peak = lax.optimization_barrier(jnp.max(masked, axis=1))
        total = lax.optimization_barrier(jnp.sum(jnp.exp(masked - peak[:, None]), axis=1))
        lse = peak + jnp.log(total)
        possum = lax.optimization_barrier(jnp.sum(jnp.where(positive, scores, jnp.float32(0.0)), axis=1))
        count = lax.optimization_barrier(jnp.sum(positive.astype(jnp.float32), axis=1))
        return (lse, possum, count)
    lse, possum, count = lax.map(stats, starts)
    lse = lse.reshape(N)
    possum = possum.reshape(N)
    count = count.reshape(N)
    loss = jnp.sum(lse - possum / count) / N

    def grads(carry, start):
        queries, scores, masked, positive = tile(start)
        block_lse = lax.dynamic_slice_in_dim(lse, start, block, 0)
        block_inv = 1.0 / lax.dynamic_slice_in_dim(count, start, block, 0)
        weight = (jnp.exp(masked - block_lse[:, None]) - jnp.where(positive, block_inv[:, None], jnp.float32(0.0))) / N
        weight = weight.astype(jnp.bfloat16)
        carry = carry + lax.dot_general(weight, queries, (((0,), (0,)), ((), ())), preferred_element_type=jnp.float32)
        rows_part = jnp.dot(weight, embeddings, preferred_element_type=jnp.float32)
        return (carry, rows_part)
    cols_part, rows_part = lax.scan(grads, jnp.zeros((N, D), jnp.float32), starts)
    grad = (scale * (rows_part.reshape(N, D) + cols_part)).astype(jnp.bfloat16)
    return (loss, grad)
```

```python
import functools

import jax
import jax.numpy as jnp
from jax import lax
from jax.experimental import pallas as pl
from jax.experimental.pallas import tpu as pltpu
from jax.sharding import Mesh
from jax.sharding import PartitionSpec as P

MESH = pl.DeviceIdType.MESH
ALL = ("y", "z", "x", "c")
IDS = 128
HALF = 32
LANES = 128


def wait_bytes(ref, sem):
    pltpu.make_async_copy(ref, ref, sem).wait()


def kernel(
    sizes,
    emb_ref,
    ids_ref,
    loss_ref,
    grad_ref,
    keys,
    queries,
    ids_smem,
    col_mine,
    col_all,
    row_mine,
    row_all,
    part_mine,
    part_all,
    loss_mine,
    loss_all,
    in_sem,
    key_send,
    key_recv,
    fwd_send,
    fwd_recv,
    query_send,
    query_recv,
    col_sem,
    row_sem,
    part_sem,
    loss_sem,
):
    ny, nz, nx, nc, rows, width = sizes
    chips = ny * nx
    plane = chips * nc
    n_query, n_key = nz * rows, plane * rows
    whole = n_query * plane
    y, z, x, c = (lax.axis_index(a) for a in ALL)
    chip = y * nx + x
    mine = chip * nc + c
    sibling = (y, z, x, 1 - c)

    def in_plane(k):
        return (k // (nx * nc), z, (k // nc) % nx, k % nc)

    def key_slot(k):
        return keys.at[pl.ds(pl.multiple_of(k * rows, rows), rows)]

    def query_slot(k):
        return queries.at[pl.ds(pl.multiple_of(k * rows, rows), rows)]

    load = pltpu.make_async_copy(emb_ref, key_slot(mine).at[:, pl.ds(0, width)], in_sem.at[0])
    load.start()
    load_ids = pltpu.make_async_copy(ids_ref, ids_smem, in_sem.at[1])
    load_ids.start()

    with jax.named_scope("barrier"):
        barrier = pltpu.get_barrier_semaphore()

        def greet_plane(k, _):
            pl.semaphore_signal(
                barrier, inc=1, device_id=in_plane(lax.rem(mine + k, plane)), device_id_type=MESH
            )
            return 0

        def greet_ring(k, _):
            pl.semaphore_signal(
                barrier, inc=1, device_id=(y, lax.rem(z + k, nz), x, c), device_id_type=MESH
            )
            return 0

        lax.fori_loop(1, plane, greet_plane, 0)
        lax.fori_loop(1, nz, greet_ring, 0)

        load_ids.wait()
        at_row = lax.broadcasted_iota(jnp.int32, (rows, IDS), 0)
        lane = lax.broadcasted_iota(jnp.int32, (rows, IDS), 1)
        ids = jnp.zeros((rows, IDS), jnp.int32)
        for r in range(rows):
            ids = jnp.where(at_row == r, ids_smem[r], ids)
        hot = jnp.logical_or(
            lane == lax.shift_right_logical(ids, 5), lane == HALF + jnp.bitwise_and(ids, HALF - 1)
        )
        key_slot(mine)[:, width:] = jnp.where(hot, 1.0, 0.0).astype(jnp.bfloat16)
        load.wait()
        query_slot(z)[...] = key_slot(mine)[...]
        pl.semaphore_wait(barrier, plane - 1 + nz - 1)

    def query_copy(k):
        return pltpu.make_async_remote_copy(
            src_ref=key_slot(mine),
            dst_ref=query_slot(z),
            send_sem=query_send.at[k],
            recv_sem=query_recv.at[k],
            device_id=(y, lax.rem(z + k, nz), x, c),
            device_id_type=MESH,
        )

    def key_copy(k):
        to = lax.rem(chip + k, chips)
        return pltpu.make_async_remote_copy(
            src_ref=key_slot(mine),
            dst_ref=key_slot(mine),
            send_sem=key_send.at[k],
            recv_sem=key_recv.at[k],
            device_id=(to // nx, z, to % nx, c),
            device_id_type=MESH,
        )

    def passed_on(k):
        slot = key_slot(lax.rem(chip + chips - k, chips) * nc + c)
        return pltpu.make_async_remote_copy(
            src_ref=slot,
            dst_ref=slot,
            send_sem=fwd_send.at[k],
            recv_sem=fwd_recv.at[k],
            device_id=sibling,
            device_id_type=MESH,
        )

    def started(copy):
        def body(k, _):
            copy(k).start()
            return 0

        return body

    with jax.named_scope("gather_start"):
        passed_on(0).start()
        lax.fori_loop(1, nz, started(query_copy), 0)
        lax.fori_loop(1, chips, started(key_copy), 0)

    with jax.named_scope("gather_pass_on"):

        def pass_on(k, _):
            key_copy(k).wait_recv()
            passed_on(k).start()
            return 0

        lax.fori_loop(1, chips, pass_on, 0)

    with jax.named_scope("gather_wait"):

        def arrived(copy):
            def body(k, _):
                copy(k).wait_recv()
                return 0

            return body

        lax.fori_loop(1, nz, arrived(query_copy), 0)
        lax.fori_loop(0, chips, arrived(passed_on), 0)

    contract_last = (((1,), (1,)), ((), ()))
    with jax.named_scope("scores"):
        scores = lax.dot_general(
            queries[:, :width], keys[:, :width], contract_last, preferred_element_type=jnp.float32
        ) * (1.0 / width**0.5)
        same = (
            lax.dot_general(
                queries[:, width:],
                keys[:, width:],
                contract_last,
                preferred_element_type=jnp.float32,
            )
            > 1.5
        )
        q_at = lax.broadcasted_iota(jnp.int32, (n_query, n_key), 0)
        k_at = lax.broadcasted_iota(jnp.int32, (n_query, n_key), 1)
        selfs = jnp.logical_and(k_at - q_at == rows * (mine - z), q_at // rows == z)
        positive = jnp.logical_and(same, jnp.logical_not(selfs))
        pos = jnp.where(positive, 1.0, 0.0)
        masked = jnp.where(selfs, jnp.float32(-1e30), scores)

    with jax.named_scope("stats"):
        peak = jnp.max(masked, axis=0, keepdims=True)
        col_lse = peak + jnp.log(jnp.sum(jnp.exp(masked - peak), axis=0, keepdims=True))
        col_count = jnp.sum(pos, axis=0, keepdims=True)
        for r in range(n_key // LANES):
            at = slice(r * LANES, (r + 1) * LANES)
            col_mine[0, r : r + 1, :] = col_lse[:, at]
            col_mine[1, r : r + 1, :] = col_count[:, at]
        col_all[pl.ds(mine, 1)] = col_mine[...][None]

    def col_copy(k):
        return pltpu.make_async_remote_copy(
            src_ref=col_mine,
            dst_ref=col_all.at[mine],
            send_sem=col_sem.at[0],
            recv_sem=col_sem.at[1],
            device_id=in_plane(lax.rem(mine + k, plane)),
            device_id_type=MESH,
        )

    def row_copy(k):
        return pltpu.make_async_remote_copy(
            src_ref=row_mine,
            dst_ref=row_all.at[z],
            send_sem=row_sem.at[0],
            recv_sem=row_sem.at[1],
            device_id=(y, lax.rem(z + k, nz), x, c),
            device_id_type=MESH,
        )

    with jax.named_scope("col_start"):
        lax.fori_loop(1, plane, started(col_copy), 0)

    with jax.named_scope("row_stats"):
        peak = jnp.max(masked, axis=1, keepdims=True)
        row_lse = peak + jnp.log(jnp.sum(jnp.exp(masked - peak), axis=1, keepdims=True))
        row_possum = jnp.sum(pos * scores, axis=1, keepdims=True)
        row_count = jnp.sum(pos, axis=1, keepdims=True)
        lane = lax.broadcasted_iota(jnp.int32, (n_query, LANES), 1)
        tall = jnp.where(lane == 0, row_lse, jnp.where(lane == 1, row_possum, row_count))
        row_mine[...] = jnp.transpose(tall)[:4]
        row_all[pl.ds(z, 1)] = row_mine[...][None]
        lax.fori_loop(1, nz, started(row_copy), 0)

    with jax.named_scope("stats_wait"):
        wait_bytes(col_all.at[pl.ds(0, plane - 1)], col_sem.at[1])
        wait_bytes(row_all.at[pl.ds(0, nz - 1)], row_sem.at[1])

    def log_sum_exp(parts):
        peak = jnp.max(parts, axis=0)
        return peak + jnp.log(jnp.sum(jnp.exp(parts - peak[None]), axis=0))

    with jax.named_scope("weights"):
        key_lse = log_sum_exp(col_all[:, 0])
        key_inverse = 1.0 / jnp.sum(col_all[:, 1], axis=0)
        query_lse = log_sum_exp(row_all[:, 0:1])
        query_possum = jnp.sum(row_all[:, 1:2], axis=0)
        query_inverse = 1.0 / jnp.sum(row_all[:, 2:3], axis=0)
        tall_lse = jnp.transpose(jnp.broadcast_to(query_lse, (LANES, n_query)))[:, :1]
        tall_inverse = jnp.transpose(jnp.broadcast_to(query_inverse, (LANES, n_query)))[:, :1]
        flat_lse = jnp.concatenate([key_lse[r : r + 1] for r in range(n_key // LANES)], axis=1)
        flat_inverse = jnp.concatenate(
            [key_inverse[r : r + 1] for r in range(n_key // LANES)], axis=1
        )
        weight = (jnp.exp(masked - tall_lse) - pos * tall_inverse) * (1.0 / whole)
        mirrored = (jnp.exp(masked - flat_lse) - pos * flat_inverse) * (1.0 / whole)

    with jax.named_scope("gradient"):
        both = jnp.concatenate([weight.astype(jnp.bfloat16), mirrored.astype(jnp.bfloat16)], axis=0)
        terms = jnp.dot(both, keys[:, :width], preferred_element_type=jnp.float32)
        terms = (terms[:n_query] + terms[n_query:]) * (1.0 / width**0.5)
        part_mine[...] = terms.astype(jnp.bfloat16)

    def part_copy(k):
        to = lax.rem(z + k, nz)
        return pltpu.make_async_remote_copy(
            src_ref=part_mine.at[pl.ds(pl.multiple_of(to * rows, rows), rows)],
            dst_ref=part_all.at[z],
            send_sem=part_sem.at[0],
            recv_sem=part_sem.at[1],
            device_id=(y, to, x, c),
            device_id_type=MESH,
        )

    def loss_copy(k):
        return pltpu.make_async_remote_copy(
            src_ref=loss_mine,
            dst_ref=loss_all.at[mine],
            send_sem=loss_sem.at[0],
            recv_sem=loss_sem.at[1],
            device_id=in_plane(lax.rem(mine + k, plane)),
            device_id_type=MESH,
        )

    with jax.named_scope("reduce_start"):
        lax.fori_loop(1, nz, started(part_copy), 0)
        part_all[pl.ds(z, 1)] = part_mine[pl.ds(pl.multiple_of(z * rows, rows), rows), :][None]
        loss_mine[...] = query_lse - query_possum * query_inverse
        loss_all[pl.ds(mine, 1)] = loss_mine[...][None]
        lax.fori_loop(1, plane, started(loss_copy), 0)

    with jax.named_scope("sends_wait"):

        def sent(copy):
            def body(k, _):
                copy(k).wait_send()
                return 0

            return body

        lax.fori_loop(1, nz, sent(query_copy), 0)
        lax.fori_loop(1, chips, sent(key_copy), 0)
        lax.fori_loop(0, chips, sent(passed_on), 0)
        wait_bytes(col_all.at[pl.ds(0, plane - 1)], col_sem.at[0])
        wait_bytes(row_all.at[pl.ds(0, nz - 1)], row_sem.at[0])
        wait_bytes(part_all.at[pl.ds(0, nz - 1)], part_sem.at[0])
        wait_bytes(loss_all.at[pl.ds(0, plane - 1)], loss_sem.at[0])

    with jax.named_scope("loss_wait"):
        wait_bytes(loss_all.at[pl.ds(0, plane - 1)], loss_sem.at[1])
        total = jnp.sum(loss_all[...], axis=0)
        loss_ref[...] = jnp.sum(total, axis=1, keepdims=True) * (1.0 / whole)

    with jax.named_scope("reduce_wait"):
        wait_bytes(part_all.at[pl.ds(0, nz - 1)], part_sem.at[1])
        grad_ref[...] = jnp.sum(part_all[...].astype(jnp.float32), axis=0).astype(jnp.bfloat16)


def on_device(embeddings, group_ids):
    ny, nz, nx, nc = (lax.axis_size(a) for a in ALL)
    rows, width = embeddings.shape
    chips = ny * nx
    plane = chips * nc
    n_query, n_key = nz * rows, plane * rows
    dma = pltpu.SemaphoreType.DMA
    loss, grad = pl.pallas_call(
        functools.partial(kernel, (ny, nz, nx, nc, rows, width)),
        out_shape=(
            jax.ShapeDtypeStruct((1, 1), jnp.float32),
            jax.ShapeDtypeStruct((rows, width), jnp.bfloat16),
        ),
        in_specs=[pl.BlockSpec(memory_space=pl.ANY)] * 2,
        out_specs=(
            pl.BlockSpec(memory_space=pltpu.VMEM),
            pl.BlockSpec(memory_space=pltpu.VMEM),
        ),
        scratch_shapes=[
            pltpu.VMEM((n_key, width + IDS), jnp.bfloat16),
            pltpu.VMEM((n_query, width + IDS), jnp.bfloat16),
            pltpu.SMEM((rows,), jnp.int32),
            pltpu.VMEM((2, n_key // LANES, LANES), jnp.float32),
            pltpu.VMEM((plane, 2, n_key // LANES, LANES), jnp.float32),
            pltpu.VMEM((4, n_query), jnp.float32),
            pltpu.VMEM((nz, 4, n_query), jnp.float32),
            pltpu.VMEM((n_query, width), jnp.bfloat16),
            pltpu.VMEM((nz, rows, width), jnp.bfloat16),
            pltpu.VMEM((1, n_query), jnp.float32),
            pltpu.VMEM((plane, 1, n_query), jnp.float32),
            dma((2,)),
            dma((chips,)),
            dma((chips,)),
            dma((chips,)),
            dma((chips,)),
            dma((nz,)),
            dma((nz,)),
            dma((2,)),
            dma((2,)),
            dma((2,)),
            dma((2,)),
        ],
        compiler_params=pltpu.CompilerParams(
            collective_id=0, has_side_effects=True, vmem_limit_bytes=32 * 1024 * 1024
        ),
    )(embeddings, group_ids)
    return loss.reshape(()), grad


def solution(mesh):
    split = Mesh(mesh.devices.reshape(4, 8, 4, 2), ALL)
    return jax.shard_map(
        on_device,
        mesh=split,
        in_specs=(P(ALL, None), P(ALL)),
        out_specs=(P(), P(ALL, None)),
        check_vma=False,
    )
```

```python
import functools

import jax
import jax.numpy as jnp
from jax import lax
from jax.experimental import pallas as pl
from jax.experimental.pallas import tpu as pltpu
from jax.sharding import Mesh
from jax.sharding import PartitionSpec as P

MESH = pl.DeviceIdType.MESH
ALL = ("y", "z", "x", "c")
IDS = 128
HALF = 32
LANES = 128


def wait_bytes(ref, sem):
    pltpu.make_async_copy(ref, ref, sem).wait()


def kernel(
    sizes,
    emb_ref,
    ids_ref,
    loss_ref,
    grad_ref,
    keys,
    queries,
    ids_smem,
    col_mine,
    col_all,
    row_mine,
    row_all,
    part_mine,
    part_all,
    loss_mine,
    loss_all,
    in_sem,
    key_send,
    key_recv,
    fwd_send,
    fwd_recv,
    query_send,
    query_recv,
    col_sem,
    row_sem,
    part_sem,
    loss_sem,
):
    ny, nz, nx, nc, rows, width = sizes
    chips = ny * nx
    plane = chips * nc
    n_query, n_key = nz * rows, plane * rows
    whole = n_query * plane
    y, z, x, c = (lax.axis_index(a) for a in ALL)
    chip = y * nx + x
    mine = chip * nc + c
    sibling = (y, z, x, 1 - c)

    ring = sorted(range(1, nz), key=lambda k: -min(k, nz - k))
    others = [(dy, dx, dc) for dy in range(ny) for dx in range(nx) for dc in range(nc)][1:]
    others.sort(key=lambda o: -min(o[0], ny - o[0]) - min(o[1], nx - o[1]))
    chips_away = [(dy, dx) for dy, dx, dc in others if dc == 0]

    def in_ring(k):
        return (y, (z + k) % nz, x, c)

    def in_plane(offset):
        dy, dx, dc = offset
        return ((y + dy) % ny, z, (x + dx) % nx, c if dc == 0 else 1 - c)

    def key_slot(k):
        return keys.at[pl.ds(pl.multiple_of(k * rows, rows), rows)]

    def query_slot(k):
        return queries.at[pl.ds(pl.multiple_of(k * rows, rows), rows)]

    load = pltpu.make_async_copy(emb_ref, key_slot(mine).at[:, pl.ds(0, width)], in_sem.at[0])
    load.start()
    load_ids = pltpu.make_async_copy(ids_ref, ids_smem, in_sem.at[1])
    load_ids.start()

    with jax.named_scope("barrier"):
        barrier = pltpu.get_barrier_semaphore()

        for k in ring[:1]:
            pl.semaphore_signal(barrier, inc=1, device_id=in_ring(k), device_id_type=MESH)
        for offset in others:
            pl.semaphore_signal(barrier, inc=1, device_id=in_plane(offset), device_id_type=MESH)
        for k in ring[1:]:
            pl.semaphore_signal(barrier, inc=1, device_id=in_ring(k), device_id_type=MESH)

        load_ids.wait()
        at_row = lax.broadcasted_iota(jnp.int32, (rows, IDS), 0)
        lane = lax.broadcasted_iota(jnp.int32, (rows, IDS), 1)
        ids = jnp.zeros((rows, IDS), jnp.int32)
        for r in range(rows):
            ids = jnp.where(at_row == r, ids_smem[r], ids)
        hot = jnp.logical_or(
            lane == lax.shift_right_logical(ids, 5), lane == HALF + jnp.bitwise_and(ids, HALF - 1)
        )
        key_slot(mine)[:, width:] = jnp.where(hot, 1.0, 0.0).astype(jnp.bfloat16)
        load.wait()
        query_slot(z)[...] = key_slot(mine)[...]
        pl.semaphore_wait(barrier, plane - 1 + nz - 1)

    def query_copy(k):
        return pltpu.make_async_remote_copy(
            src_ref=key_slot(mine),
            dst_ref=query_slot(z),
            send_sem=query_send.at[k],
            recv_sem=query_recv.at[k],
            device_id=in_ring(k),
            device_id_type=MESH,
        )

    def key_copy(offset):
        return pltpu.make_async_remote_copy(
            src_ref=key_slot(mine),
            dst_ref=key_slot(mine),
            send_sem=key_send.at[offset[0] * nx + offset[1]],
            recv_sem=key_recv.at[offset[0] * nx + offset[1]],
            device_id=in_plane((*offset, 0)),
            device_id_type=MESH,
        )

    def passed_on(offset):
        came_from = (y + ny - offset[0]) % ny * nx + (x + nx - offset[1]) % nx
        slot = key_slot(came_from * nc + c)
        return pltpu.make_async_remote_copy(
            src_ref=slot,
            dst_ref=slot,
            send_sem=fwd_send.at[offset[0] * nx + offset[1]],
            recv_sem=fwd_recv.at[offset[0] * nx + offset[1]],
            device_id=sibling,
            device_id_type=MESH,
        )

    with jax.named_scope("gather_start"):
        query_copy(ring[0]).start()
        for offset in chips_away[:5]:
            key_copy(offset).start()
        for k in ring[1:]:
            query_copy(k).start()
        for offset in chips_away[5:]:
            key_copy(offset).start()
        passed_on((0, 0)).start()

    with jax.named_scope("key_pass_on"):
        for offset in chips_away[::-1]:
            key_copy(offset).wait_recv()
            passed_on(offset).start()

    with jax.named_scope("gather_wait"):
        for k in ring[::-1]:
            query_copy(k).wait_recv()
        for offset in [(0, 0)] + chips_away[::-1]:
            passed_on(offset).wait_recv()

    contract_last = (((1,), (1,)), ((), ()))
    with jax.named_scope("scores"):
        scores = lax.dot_general(
            queries[:, :width], keys[:, :width], contract_last, preferred_element_type=jnp.float32
        ) * (1.0 / width**0.5)
        same = (
            lax.dot_general(
                queries[:, width:],
                keys[:, width:],
                contract_last,
                preferred_element_type=jnp.float32,
            )
            > 1.5
        )
        q_at = lax.broadcasted_iota(jnp.int32, (n_query, n_key), 0)
        k_at = lax.broadcasted_iota(jnp.int32, (n_query, n_key), 1)
        selfs = jnp.logical_and(k_at - q_at == rows * (mine - z), q_at // rows == z)
        positive = jnp.logical_and(same, jnp.logical_not(selfs))
        pos = jnp.where(positive, 1.0, 0.0)
        masked = jnp.where(selfs, jnp.float32(-1e30), scores)

    with jax.named_scope("stats"):
        peak = jnp.max(masked, axis=0, keepdims=True)
        col_lse = peak + jnp.log(jnp.sum(jnp.exp(masked - peak), axis=0, keepdims=True))
        col_count = jnp.sum(pos, axis=0, keepdims=True)
        for r in range(n_key // LANES):
            at = slice(r * LANES, (r + 1) * LANES)
            col_mine[0, r : r + 1, :] = col_lse[:, at]
            col_mine[1, r : r + 1, :] = col_count[:, at]
        col_all[pl.ds(mine, 1)] = col_mine[...][None]

    def col_copy(offset):
        return pltpu.make_async_remote_copy(
            src_ref=col_mine,
            dst_ref=col_all.at[mine],
            send_sem=col_sem.at[0],
            recv_sem=col_sem.at[1],
            device_id=in_plane(offset),
            device_id_type=MESH,
        )

    def row_copy(k):
        return pltpu.make_async_remote_copy(
            src_ref=row_mine,
            dst_ref=row_all.at[z],
            send_sem=row_sem.at[0],
            recv_sem=row_sem.at[1],
            device_id=in_ring(k),
            device_id_type=MESH,
        )

    with jax.named_scope("col_start"):
        for offset in others:
            col_copy(offset).start()

    with jax.named_scope("row_stats"):
        peak = jnp.max(masked, axis=1, keepdims=True)
        row_lse = peak + jnp.log(jnp.sum(jnp.exp(masked - peak), axis=1, keepdims=True))
        row_possum = jnp.sum(pos * scores, axis=1, keepdims=True)
        row_count = jnp.sum(pos, axis=1, keepdims=True)
        lane = lax.broadcasted_iota(jnp.int32, (n_query, LANES), 1)
        tall = jnp.where(lane == 0, row_lse, jnp.where(lane == 1, row_possum, row_count))
        row_mine[...] = jnp.transpose(tall)[:4]
        row_all[pl.ds(z, 1)] = row_mine[...][None]
        for k in ring:
            row_copy(k).start()

    with jax.named_scope("stats_wait"):
        wait_bytes(col_all.at[pl.ds(0, plane - 1)], col_sem.at[1])
        wait_bytes(row_all.at[pl.ds(0, nz - 1)], row_sem.at[1])

    def log_sum_exp(parts):
        peak = jnp.max(parts, axis=0)
        return peak + jnp.log(jnp.sum(jnp.exp(parts - peak[None]), axis=0))

    with jax.named_scope("weights"):
        key_lse = log_sum_exp(col_all[:, 0])
        key_inverse = 1.0 / jnp.sum(col_all[:, 1], axis=0)
        query_lse = log_sum_exp(row_all[:, 0:1])
        query_possum = jnp.sum(row_all[:, 1:2], axis=0)
        query_inverse = 1.0 / jnp.sum(row_all[:, 2:3], axis=0)
        tall_lse = jnp.transpose(jnp.broadcast_to(query_lse, (LANES, n_query)))[:, :1]
        tall_inverse = jnp.transpose(jnp.broadcast_to(query_inverse, (LANES, n_query)))[:, :1]
        flat_lse = jnp.concatenate([key_lse[r : r + 1] for r in range(n_key // LANES)], axis=1)
        flat_inverse = jnp.concatenate(
            [key_inverse[r : r + 1] for r in range(n_key // LANES)], axis=1
        )
        weight = (jnp.exp(masked - tall_lse) - pos * tall_inverse) * (1.0 / whole)
        mirrored = (jnp.exp(masked - flat_lse) - pos * flat_inverse) * (1.0 / whole)

    with jax.named_scope("gradient"):
        both = jnp.concatenate([weight.astype(jnp.bfloat16), mirrored.astype(jnp.bfloat16)], axis=0)
        terms = jnp.dot(both, keys[:, :width], preferred_element_type=jnp.float32)
        terms = (terms[:n_query] + terms[n_query:]) * (1.0 / width**0.5)
        part_mine[...] = terms.astype(jnp.bfloat16)

    def part_copy(to):
        return pltpu.make_async_remote_copy(
            src_ref=part_mine.at[pl.ds(to * rows, rows)],
            dst_ref=part_all.at[z],
            send_sem=part_sem.at[0],
            recv_sem=part_sem.at[1],
            device_id=(y, to, x, c),
            device_id_type=MESH,
        )

    def loss_copy(offset):
        return pltpu.make_async_remote_copy(
            src_ref=loss_mine,
            dst_ref=loss_all.at[mine],
            send_sem=loss_sem.at[0],
            recv_sem=loss_sem.at[1],
            device_id=in_plane(offset),
            device_id_type=MESH,
        )

    with jax.named_scope("reduce_start"):
        for to in range(nz):

            @pl.when(z != to)
            def _():
                part_copy(to).start()

        part_all[pl.ds(z, 1)] = part_mine[pl.ds(pl.multiple_of(z * rows, rows), rows), :][None]

    with jax.named_scope("loss_start"):
        loss_mine[...] = query_lse - query_possum * query_inverse
        loss_all[pl.ds(mine, 1)] = loss_mine[...][None]
        for offset in others:
            loss_copy(offset).start()

    with jax.named_scope("gather_sent"):
        for k in ring:
            query_copy(k).wait_send()
        for offset in chips_away:
            key_copy(offset).wait_send()
        for offset in [(0, 0)] + chips_away:
            passed_on(offset).wait_send()

    with jax.named_scope("stats_sent"):
        wait_bytes(col_all.at[pl.ds(0, plane - 1)], col_sem.at[0])
        wait_bytes(row_all.at[pl.ds(0, nz - 1)], row_sem.at[0])

    with jax.named_scope("part_sent"):
        wait_bytes(part_all.at[pl.ds(0, nz - 1)], part_sem.at[0])

    with jax.named_scope("loss_sent"):
        wait_bytes(loss_all.at[pl.ds(0, plane - 1)], loss_sem.at[0])

    with jax.named_scope("loss_wait"):
        wait_bytes(loss_all.at[pl.ds(0, plane - 1)], loss_sem.at[1])
        total = jnp.sum(loss_all[...], axis=0)
        loss_ref[...] = jnp.broadcast_to(jnp.sum(total, axis=1, keepdims=True) * (1.0 / whole), (8, 128))

    with jax.named_scope("reduce_wait"):
        wait_bytes(part_all.at[pl.ds(0, nz - 1)], part_sem.at[1])
        grad_ref[...] = jnp.sum(part_all[...].astype(jnp.float32), axis=0).astype(jnp.bfloat16)


def on_device(embeddings, group_ids):
    ny, nz, nx, nc = (lax.axis_size(a) for a in ALL)
    rows, width = embeddings.shape
    chips = ny * nx
    plane = chips * nc
    n_query, n_key = nz * rows, plane * rows
    dma = pltpu.SemaphoreType.DMA
    loss, grad = pl.pallas_call(
        functools.partial(kernel, (ny, nz, nx, nc, rows, width)),
        out_shape=(
            pltpu.VMEM((8, 128), jnp.float32),
            pltpu.VMEM((rows, width), jnp.bfloat16),
        ),
        in_specs=[pl.BlockSpec(memory_space=pltpu.HBM)] * 2,
        out_specs=(
            pl.BlockSpec(memory_space=pltpu.VMEM),
            pl.BlockSpec(memory_space=pltpu.VMEM),
        ),
        scratch_shapes=[
            pltpu.VMEM((n_key, width + IDS), jnp.bfloat16),
            pltpu.VMEM((n_query, width + IDS), jnp.bfloat16),
            pltpu.SMEM((rows,), jnp.int32),
            pltpu.VMEM((2, n_key // LANES, LANES), jnp.float32),
            pltpu.VMEM((plane, 2, n_key // LANES, LANES), jnp.float32),
            pltpu.VMEM((4, n_query), jnp.float32),
            pltpu.VMEM((nz, 4, n_query), jnp.float32),
            pltpu.VMEM((n_query, width), jnp.bfloat16),
            pltpu.VMEM((nz, rows, width), jnp.bfloat16),
            pltpu.VMEM((1, n_query), jnp.float32),
            pltpu.VMEM((plane, 1, n_query), jnp.float32),
            dma((2,)),
            dma((chips,)),
            dma((chips,)),
            dma((chips,)),
            dma((chips,)),
            dma((nz,)),
            dma((nz,)),
            dma((2,)),
            dma((2,)),
            dma((2,)),
            dma((2,)),
        ],
        compiler_params=pltpu.CompilerParams(
            collective_id=0, has_side_effects=True, vmem_limit_bytes=60 * 1024 * 1024
        ),
    )(embeddings, group_ids)

    def finish(loss_in, grad_in, loss_out, grad_out):
        loss_out[...] = loss_in[:1, :1]
        grad_out[...] = grad_in[...]

    loss, grad = pl.pallas_call(
        finish,
        out_shape=(
            jax.ShapeDtypeStruct((1, 1), jnp.float32),
            jax.ShapeDtypeStruct((rows, width), jnp.bfloat16),
        ),
        in_specs=[pl.BlockSpec(memory_space=pltpu.VMEM)] * 2,
        compiler_params=pltpu.CompilerParams(vmem_limit_bytes=1024 * 1024),
    )(loss, grad)
    return loss.reshape(()), grad


def solution(mesh):
    split = Mesh(mesh.devices.reshape(4, 8, 4, 2), ALL)
    return jax.shard_map(
        on_device,
        mesh=split,
        in_specs=(P(ALL, None), P(ALL)),
        out_specs=(P(), P(ALL, None)),
        check_vma=False,
    )
```

```python
import functools

import jax
import jax.numpy as jnp
from jax import lax
from jax.experimental import pallas as pl
from jax.experimental.pallas import tpu as pltpu
from jax.sharding import Mesh
from jax.sharding import PartitionSpec as P

MESH = pl.DeviceIdType.MESH
ALL = ("y", "z", "x", "c")
LANES = 128


def wait_bytes(ref, sem):
    pltpu.make_async_copy(ref, ref, sem).wait()


def kernel(
    sizes,
    emb_ref,
    ids_ref,
    loss_ref,
    grad_ref,
    keys,
    queries,
    ids_smem,
    ids_mine,
    ids_plane,
    ids_ring,
    col_mine,
    col_all,
    row_mine,
    row_all,
    part_mine,
    part_all,
    loss_mine,
    loss_all,
    in_sem,
    key_send,
    key_recv,
    fwd_send,
    fwd_recv,
    query_send,
    query_recv,
    ids_plane_sem,
    ids_ring_sem,
    col_sem,
    row_sem,
    part_sem,
    loss_sem,
):
    ny, nz, nx, nc, rows, width = sizes
    chips = ny * nx
    plane = chips * nc
    n_query, n_key, n_half = nz * rows, plane * rows, chips * rows
    whole = n_query * plane
    y, z, x, c = (lax.axis_index(a) for a in ALL)
    chip = y * nx + x
    sibling = (y, z, x, 1 - c)

    ring = sorted(range(1, nz), key=lambda k: -min(k, nz - k))
    others = [(dy, dx, dc) for dy in range(ny) for dx in range(nx) for dc in range(nc)][1:]
    others.sort(key=lambda o: -min(o[0], ny - o[0]) - min(o[1], nx - o[1]))
    chips_away = [(dy, dx) for dy, dx, dc in others if dc == 0]

    def in_ring(k):
        return (y, (z + k) % nz, x, c)

    def in_plane(offset):
        dy, dx, dc = offset
        return ((y + dy) % ny, z, (x + dx) % nx, c if dc == 0 else 1 - c)

    def key_slot(half, k):
        start = half * n_half + pl.multiple_of(k * rows, rows)
        return keys.at[pl.ds(start, rows)]

    def query_slot(k):
        return queries.at[pl.ds(pl.multiple_of(k * rows, rows), rows)]

    load = pltpu.make_async_copy(emb_ref, key_slot(0, chip), in_sem.at[0])
    load.start()
    load_ids = pltpu.make_async_copy(ids_ref, ids_smem, in_sem.at[1])
    load_ids.start()

    with jax.named_scope("barrier"):
        barrier = pltpu.get_barrier_semaphore()

        for k in ring[:1]:
            pl.semaphore_signal(barrier, inc=1, device_id=in_ring(k), device_id_type=MESH)
        for offset in others:
            pl.semaphore_signal(barrier, inc=1, device_id=in_plane(offset), device_id_type=MESH)
        for k in ring[1:]:
            pl.semaphore_signal(barrier, inc=1, device_id=in_ring(k), device_id_type=MESH)

        load_ids.wait()
        lane = lax.broadcasted_iota(jnp.int32, (1, LANES), 1)
        for at, place in ((0, lax.rem(chip, LANES // rows)), (1, z)):
            line = jnp.zeros((1, LANES), jnp.int32)
            for r in range(rows):
                line = jnp.where(lane == place * rows + r, ids_smem[r], line)
            ids_mine[at] = line
        ids_plane[pl.ds(chip, 1)] = ids_mine[0:1]
        ids_ring[pl.ds(z, 1)] = ids_mine[1:2]
        load.wait()
        query_slot(z)[...] = key_slot(0, chip)[...]
        pl.semaphore_wait(barrier, plane - 1 + nz - 1)

    def query_via(k):
        if min(k, nz - k) < 3:
            return 0
        return 2 if k <= nz // 2 else nz - 2

    def query_copy(k):
        via = query_via(k)
        source = (z + nz - via) % nz
        return pltpu.make_async_remote_copy(
            src_ref=query_slot(source) if via else key_slot(0, chip),
            dst_ref=query_slot(source),
            send_sem=query_send.at[k],
            recv_sem=query_recv.at[k],
            device_id=in_ring((k + nz - via) % nz),
            device_id_type=MESH,
        )

    def key_via(offset):
        dy, dx = offset
        if dy == 0 or dx == 0:
            return (0, 0)
        if min(dy, ny - dy) == min(dx, nx - dx):
            return (dy, 0) if dy == dx else (0, dx)
        return (dy, 0) if min(dy, ny - dy) == 2 else (0, dx)

    def key_copy(offset):
        at = offset[0] * nx + offset[1]
        via = key_via(offset)
        source = (y + ny - via[0]) % ny * nx + (x + nx - via[1]) % nx
        onward = ((offset[0] + ny - via[0]) % ny, (offset[1] + nx - via[1]) % nx)
        return pltpu.make_async_remote_copy(
            src_ref=key_slot(0, source),
            dst_ref=key_slot(0, source),
            send_sem=key_send.at[at],
            recv_sem=key_recv.at[at],
            device_id=in_plane((*onward, 0)),
            device_id_type=MESH,
        )

    def passed_on(offset):
        at = offset[0] * nx + offset[1]
        came_from = (y + ny - offset[0]) % ny * nx + (x + nx - offset[1]) % nx
        return pltpu.make_async_remote_copy(
            src_ref=key_slot(0, came_from),
            dst_ref=key_slot(1, came_from),
            send_sem=fwd_send.at[at],
            recv_sem=fwd_recv.at[at],
            device_id=sibling,
            device_id_type=MESH,
        )

    def ids_plane_copy(offset):
        return pltpu.make_async_remote_copy(
            src_ref=ids_mine.at[0],
            dst_ref=ids_plane.at[offset[2] * chips + chip],
            send_sem=ids_plane_sem.at[0],
            recv_sem=ids_plane_sem.at[1],
            device_id=in_plane(offset),
            device_id_type=MESH,
        )

    def ids_ring_copy(k):
        return pltpu.make_async_remote_copy(
            src_ref=ids_mine.at[1],
            dst_ref=ids_ring.at[z],
            send_sem=ids_ring_sem.at[0],
            recv_sem=ids_ring_sem.at[1],
            device_id=in_ring(k),
            device_id_type=MESH,
        )

    query_direct = [k for k in ring if not query_via(k)]
    query_relays = [k for k in ring if query_via(k)]
    key_direct = [o for o in chips_away if not any(key_via(o))]
    key_direct.sort(key=lambda o: 0 if 2 in o else 1 if 0 not in o else 2)
    key_relays = [o for o in chips_away if any(key_via(o))]

    with jax.named_scope("gather_start"):
        for offset in key_direct[:2]:
            key_copy(offset).start()
        for k in query_direct[:2]:
            query_copy(k).start()
        for offset in key_direct[2:]:
            key_copy(offset).start()
        for k in query_direct[2:]:
            query_copy(k).start()
        passed_on((0, 0)).start()
        for offset in others:
            ids_plane_copy(offset).start()
        for k in ring:
            ids_ring_copy(k).start()

    with jax.named_scope("gather_relay"):
        for offset in key_direct[2:] + key_direct[:2]:
            key_copy(offset).wait_recv()
            for further in key_relays:
                if key_via(further) == offset:
                    key_copy(further).start()
            passed_on(offset).start()
        for k in query_direct[:2]:
            query_copy(k).wait_recv()
            for further in query_relays:
                if query_via(further) == k:
                    query_copy(further).start()

    with jax.named_scope("key_pass_on"):
        for offset in key_relays[::-1]:
            key_copy(offset).wait_recv()
            passed_on(offset).start()

    with jax.named_scope("query_wait"):
        for k in query_direct[2:] + query_relays:
            query_copy(k).wait_recv()

    def scores_with(half):
        return lax.dot_general(
            queries[...],
            keys[half * n_half : (half + 1) * n_half],
            (((1,), (1,)), ((), ())),
            preferred_element_type=jnp.float32,
        ) * (1.0 / width**0.5)

    def down_log_sum_exp(values):
        peak = jnp.max(values, axis=0, keepdims=True)
        return peak + jnp.log(jnp.sum(jnp.exp(values - peak), axis=0, keepdims=True))

    with jax.named_scope("own_scores"):
        scores_own = scores_with(0)
        q_at = lax.broadcasted_iota(jnp.int32, (n_query, n_half), 0)
        k_at = lax.broadcasted_iota(jnp.int32, (n_query, n_half), 1)
        selfs = jnp.logical_and(k_at - q_at == rows * (chip - z), q_at // rows == z)
        masked_own = jnp.where(selfs, jnp.float32(-1e30), scores_own)
        lse_own = down_log_sum_exp(masked_own)

    with jax.named_scope("passed_wait"):
        for offset in [(0, 0)] + chips_away[::-1]:
            passed_on(offset).wait_recv()

    with jax.named_scope("scores"):
        scores_other = scores_with(1)
        masked = jnp.concatenate([masked_own, scores_other], axis=1)
        col_lse = jnp.concatenate([lse_own, down_log_sum_exp(scores_other)], axis=1)

    with jax.named_scope("positives"):
        wait_bytes(ids_plane.at[pl.ds(0, plane - 1)], ids_plane_sem.at[1])
        wait_bytes(ids_ring.at[pl.ds(0, nz - 1)], ids_ring_sem.at[1])
        query_ids = jnp.sum(ids_ring[...], axis=0)
        tall_ids = jnp.transpose(jnp.broadcast_to(query_ids, (LANES, n_query)))
        group = LANES // rows
        same = [
            tall_ids == jnp.sum(ids_plane[at : at + group], axis=0)
            for at in range(0, plane, group)
        ]
        same = jnp.concatenate([jnp.where(one, 1.0, 0.0) for one in same], axis=1)
        pos = jnp.concatenate(
            [jnp.where(selfs, 0.0, same[:, :n_half]), same[:, n_half:]], axis=1
        )

    with jax.named_scope("stats"):
        col_count = jnp.sum(pos, axis=0, keepdims=True)
        blocks = n_key // LANES
        for r in range(blocks):
            at = slice(r * LANES, (r + 1) * LANES)
            for turn in range(2):
                to = (r + turn * blocks // 2) % blocks
                col_mine[turn, 0, to : to + 1, :] = col_lse[:, at]
                col_mine[turn, 1, to : to + 1, :] = col_count[:, at]
        col_all[pl.ds(chip, 1)] = col_mine[0:1]

    def col_copy(offset):
        return pltpu.make_async_remote_copy(
            src_ref=col_mine.at[offset[2]],
            dst_ref=col_all.at[offset[2] * chips + chip],
            send_sem=col_sem.at[0],
            recv_sem=col_sem.at[1],
            device_id=in_plane(offset),
            device_id_type=MESH,
        )

    def row_copy(k):
        return pltpu.make_async_remote_copy(
            src_ref=row_mine,
            dst_ref=row_all.at[z],
            send_sem=row_sem.at[0],
            recv_sem=row_sem.at[1],
            device_id=in_ring(k),
            device_id_type=MESH,
        )

    with jax.named_scope("col_start"):
        for offset in others:
            col_copy(offset).start()

    with jax.named_scope("row_stats"):
        peak = jnp.max(masked, axis=1, keepdims=True)
        row_lse = peak + jnp.log(jnp.sum(jnp.exp(masked - peak), axis=1, keepdims=True))
        row_possum = jnp.sum(pos * masked, axis=1, keepdims=True)
        row_count = jnp.sum(pos, axis=1, keepdims=True)
        lane = lax.broadcasted_iota(jnp.int32, (n_query, LANES), 1)
        tall = jnp.where(lane == 0, row_lse, jnp.where(lane == 1, row_possum, row_count))
        row_mine[...] = jnp.transpose(tall)[:4]
        row_all[pl.ds(z, 1)] = row_mine[...][None]
        for k in ring:
            row_copy(k).start()

    with jax.named_scope("stats_wait"):
        wait_bytes(col_all.at[pl.ds(0, plane - 1)], col_sem.at[1])
        wait_bytes(row_all.at[pl.ds(0, nz - 1)], row_sem.at[1])

    def log_sum_exp(parts):
        peak = jnp.max(parts, axis=0)
        return peak + jnp.log(jnp.sum(jnp.exp(parts - peak[None]), axis=0))

    with jax.named_scope("weights"):
        key_lse = log_sum_exp(col_all[:, 0])
        key_inverse = 1.0 / jnp.sum(col_all[:, 1], axis=0)
        query_lse = log_sum_exp(row_all[:, 0:1])
        query_possum = jnp.sum(row_all[:, 1:2], axis=0)
        query_inverse = 1.0 / jnp.sum(row_all[:, 2:3], axis=0)
        tall_lse = jnp.transpose(jnp.broadcast_to(query_lse, (LANES, n_query)))[:, :1]
        tall_inverse = jnp.transpose(jnp.broadcast_to(query_inverse, (LANES, n_query)))[:, :1]
        flat_lse = jnp.concatenate([key_lse[r : r + 1] for r in range(n_key // LANES)], axis=1)
        flat_inverse = jnp.concatenate(
            [key_inverse[r : r + 1] for r in range(n_key // LANES)], axis=1
        )
        weight = (jnp.exp(masked - tall_lse) - pos * tall_inverse) * (1.0 / whole)
        mirrored = (jnp.exp(masked - flat_lse) - pos * flat_inverse) * (1.0 / whole)

    with jax.named_scope("gradient"):
        weight = weight.astype(jnp.bfloat16)
        mirrored = mirrored.astype(jnp.bfloat16)

    def part_copy(to):
        return pltpu.make_async_remote_copy(
            src_ref=part_mine.at[pl.ds(to * rows, rows)],
            dst_ref=part_all.at[z],
            send_sem=part_sem.at[0],
            recv_sem=part_sem.at[1],
            device_id=(y, to, x, c),
            device_id_type=MESH,
        )

    def loss_copy(offset):
        return pltpu.make_async_remote_copy(
            src_ref=loss_mine,
            dst_ref=loss_all.at[offset[2] * chips + chip],
            send_sem=loss_sem.at[0],
            recv_sem=loss_sem.at[1],
            device_id=in_plane(offset),
            device_id_type=MESH,
        )

    with jax.named_scope("reduce_start"):
        some = n_query // 2
        for first in range(0, n_query, some):
            last = first + some
            both = jnp.concatenate([weight[first:last], mirrored[first:last]], axis=0)
            terms = jnp.dot(both, keys[...], preferred_element_type=jnp.float32)
            terms = (terms[:some] + terms[some:]) * (1.0 / width**0.5)
            part_mine[first:last] = terms.astype(jnp.bfloat16)
            for to in range(first // rows, last // rows):

                @pl.when(z != to)
                def _():
                    part_copy(to).start()

        part_all[pl.ds(z, 1)] = part_mine[pl.ds(pl.multiple_of(z * rows, rows), rows), :][None]

    with jax.named_scope("loss_start"):
        loss_mine[...] = query_lse - query_possum * query_inverse
        loss_all[pl.ds(chip, 1)] = loss_mine[...][None]
        for offset in others:
            loss_copy(offset).start()

    with jax.named_scope("gather_sent"):
        for k in ring:
            query_copy(k).wait_send()
        for offset in chips_away:
            key_copy(offset).wait_send()
        for offset in [(0, 0)] + chips_away:
            passed_on(offset).wait_send()
        wait_bytes(ids_plane.at[pl.ds(0, plane - 1)], ids_plane_sem.at[0])
        wait_bytes(ids_ring.at[pl.ds(0, nz - 1)], ids_ring_sem.at[0])

    with jax.named_scope("stats_sent"):
        wait_bytes(col_all.at[pl.ds(0, plane - 1)], col_sem.at[0])
        wait_bytes(row_all.at[pl.ds(0, nz - 1)], row_sem.at[0])

    with jax.named_scope("part_sent"):
        wait_bytes(part_all.at[pl.ds(0, nz - 1)], part_sem.at[0])

    with jax.named_scope("loss_sent"):
        wait_bytes(loss_all.at[pl.ds(0, plane - 1)], loss_sem.at[0])

    with jax.named_scope("loss_wait"):
        wait_bytes(loss_all.at[pl.ds(0, plane - 1)], loss_sem.at[1])
        total = jnp.sum(loss_all[...], axis=0)
        loss_ref[...] = jnp.broadcast_to(jnp.sum(total, axis=1, keepdims=True) * (1.0 / whole), (8, 128))

    with jax.named_scope("reduce_wait"):
        wait_bytes(part_all.at[pl.ds(0, nz - 1)], part_sem.at[1])
        grad_ref[...] = jnp.sum(part_all[...].astype(jnp.float32), axis=0).astype(jnp.bfloat16)


def on_device(embeddings, group_ids):
    ny, nz, nx, nc = (lax.axis_size(a) for a in ALL)
    rows, width = embeddings.shape
    chips = ny * nx
    plane = chips * nc
    n_query, n_key = nz * rows, plane * rows
    dma = pltpu.SemaphoreType.DMA
    loss, grad = pl.pallas_call(
        functools.partial(kernel, (ny, nz, nx, nc, rows, width)),
        out_shape=(
            pltpu.VMEM((8, 128), jnp.float32),
            pltpu.VMEM((rows, width), jnp.bfloat16),
        ),
        in_specs=[pl.BlockSpec(memory_space=pltpu.HBM)] * 2,
        out_specs=(
            pl.BlockSpec(memory_space=pltpu.VMEM),
            pl.BlockSpec(memory_space=pltpu.VMEM),
        ),
        scratch_shapes=[
            pltpu.VMEM((n_key, width), jnp.bfloat16),
            pltpu.VMEM((n_query, width), jnp.bfloat16),
            pltpu.SMEM((rows,), jnp.int32),
            pltpu.VMEM((2, 1, LANES), jnp.int32),
            pltpu.VMEM((plane, 1, LANES), jnp.int32),
            pltpu.VMEM((nz, 1, LANES), jnp.int32),
            pltpu.VMEM((2, 2, n_key // LANES, LANES), jnp.float32),
            pltpu.VMEM((plane, 2, n_key // LANES, LANES), jnp.float32),
            pltpu.VMEM((4, n_query), jnp.float32),
            pltpu.VMEM((nz, 4, n_query), jnp.float32),
            pltpu.VMEM((n_query, width), jnp.bfloat16),
            pltpu.VMEM((nz, rows, width), jnp.bfloat16),
            pltpu.VMEM((1, n_query), jnp.float32),
            pltpu.VMEM((plane, 1, n_query), jnp.float32),
            dma((2,)),
            dma((chips,)),
            dma((chips,)),
            dma((chips,)),
            dma((chips,)),
            dma((nz,)),
            dma((nz,)),
            dma((2,)),
            dma((2,)),
            dma((2,)),
            dma((2,)),
            dma((2,)),
            dma((2,)),
        ],
        compiler_params=pltpu.CompilerParams(
            collective_id=0, has_side_effects=True, vmem_limit_bytes=60 * 1024 * 1024
        ),
    )(embeddings, group_ids)

    def finish(loss_in, grad_in, loss_out, grad_out):
        loss_out[...] = loss_in[:1, :1]
        grad_out[...] = grad_in[...]

    loss, grad = pl.pallas_call(
        finish,
        out_shape=(
            jax.ShapeDtypeStruct((1, 1), jnp.float32),
            jax.ShapeDtypeStruct((rows, width), jnp.bfloat16),
        ),
        in_specs=[pl.BlockSpec(memory_space=pltpu.VMEM)] * 2,
        compiler_params=pltpu.CompilerParams(vmem_limit_bytes=1024 * 1024),
    )(loss, grad)
    return loss.reshape(()), grad


def solution(mesh):
    split = Mesh(mesh.devices.reshape(4, 8, 4, 2), ALL)
    return jax.shard_map(
        on_device,
        mesh=split,
        in_specs=(P(ALL, None), P(ALL)),
        out_specs=(P(), P(ALL, None)),
        check_vma=False,
    )
```

```python
import functools

import jax
import jax.numpy as jnp
from jax import lax
from jax.experimental import pallas as pl
from jax.experimental.pallas import tpu as pltpu
from jax.sharding import Mesh
from jax.sharding import PartitionSpec as P

MESH = pl.DeviceIdType.MESH
ALL = ("y", "z", "x", "c")
LANES = 128
IDS = 128
HALF = 32


def wait_bytes(ref, sem):
    pltpu.make_async_copy(ref, ref, sem).wait()


def kernel(
    sizes,
    emb_ref,
    ids_ref,
    loss_ref,
    grad_ref,
    keys,
    queries,
    ids_smem,
    col_mine,
    col_all,
    row_mine,
    row_all,
    part_mine,
    part_all,
    loss_mine,
    loss_all,
    in_sem,
    key_send,
    key_recv,
    fwd_send,
    fwd_recv,
    query_send,
    query_recv,
    col_sem,
    row_sem,
    part_sem,
    loss_sem,
):
    ny, nz, nx, nc, rows, width = sizes
    chips = ny * nx
    plane = chips * nc
    n_query, n_key, n_half = nz * rows, plane * rows, chips * rows
    whole = n_query * plane
    y, z, x, c = (lax.axis_index(a) for a in ALL)
    chip = y * nx + x
    sibling = (y, z, x, 1 - c)

    ring = sorted(range(1, nz), key=lambda k: -min(k, nz - k))
    others = [(dy, dx, dc) for dy in range(ny) for dx in range(nx) for dc in range(nc)][1:]
    others.sort(key=lambda o: -min(o[0], ny - o[0]) - min(o[1], nx - o[1]))
    chips_away = [(dy, dx) for dy, dx, dc in others if dc == 0]

    def in_ring(k):
        return (y, (z + k) % nz, x, c)

    def in_plane(offset):
        dy, dx, dc = offset
        return ((y + dy) % ny, z, (x + dx) % nx, c if dc == 0 else 1 - c)

    def key_slot(half, k):
        start = half * n_half + pl.multiple_of(k * rows, rows)
        return keys.at[pl.ds(start, rows)]

    def query_via(k):
        if min(k, nz - k) < 3:
            return 0
        return 2 if k <= nz // 2 else nz - 2

    def key_via(offset):
        dy, dx = offset
        if dy == 0 or dx == 0:
            return (0, 0)
        if min(dy, ny - dy) == min(dx, nx - dx):
            return (dy, 0) if dy == dx else (0, dx)
        return (dy, 0) if min(dy, ny - dy) == 2 else (0, dx)

    query_direct = [k for k in ring if not query_via(k)]
    query_relays = [k for k in ring if query_via(k)]
    key_direct = [o for o in chips_away if not any(key_via(o))]
    key_direct.sort(key=lambda o: 0 if 2 in o else 1 if 0 not in o else 2)
    key_relays = [o for o in chips_away if any(key_via(o))]

    def query_slot(k):
        return queries.at[pl.ds(pl.multiple_of(k * rows, rows), rows)]

    load = pltpu.make_async_copy(emb_ref, key_slot(0, chip).at[:, pl.ds(0, width)], in_sem.at[0])
    load.start()
    load_ids = pltpu.make_async_copy(ids_ref, ids_smem, in_sem.at[1])
    load_ids.start()

    with jax.named_scope("barrier"):
        barrier = pltpu.get_barrier_semaphore()

        for offset in key_direct:
            pl.semaphore_signal(
                barrier, inc=1, device_id=in_plane((*offset, 0)), device_id_type=MESH
            )
        for k in query_direct:
            pl.semaphore_signal(barrier, inc=1, device_id=in_ring(k), device_id_type=MESH)
        pl.semaphore_signal(barrier, inc=1, device_id=sibling, device_id_type=MESH)

        load_ids.wait()
        at_row = lax.broadcasted_iota(jnp.int32, (rows, IDS), 0)
        lane = lax.broadcasted_iota(jnp.int32, (rows, IDS), 1)
        ids = jnp.zeros((rows, IDS), jnp.int32)
        for r in range(rows):
            ids = jnp.where(at_row == r, ids_smem[r], ids)
        hot = jnp.logical_or(
            lane == lax.shift_right_logical(ids, 5), lane == HALF + jnp.bitwise_and(ids, HALF - 1)
        )
        key_slot(0, chip)[:, width:] = jnp.where(hot, 1.0, 0.0).astype(jnp.bfloat16)
        load.wait()
        query_slot(z)[...] = key_slot(0, chip)[...]
        pl.semaphore_wait(barrier, len(key_direct) + len(query_direct) + 1)

    def query_copy(k):
        via = query_via(k)
        source = (z + nz - via) % nz
        return pltpu.make_async_remote_copy(
            src_ref=query_slot(source) if via else key_slot(0, chip),
            dst_ref=query_slot(source),
            send_sem=query_send.at[k],
            recv_sem=query_recv.at[k],
            device_id=in_ring((k + nz - via) % nz),
            device_id_type=MESH,
        )

    def key_copy(offset):
        at = offset[0] * nx + offset[1]
        via = key_via(offset)
        source = (y + ny - via[0]) % ny * nx + (x + nx - via[1]) % nx
        onward = ((offset[0] + ny - via[0]) % ny, (offset[1] + nx - via[1]) % nx)
        return pltpu.make_async_remote_copy(
            src_ref=key_slot(0, source),
            dst_ref=key_slot(0, source),
            send_sem=key_send.at[at],
            recv_sem=key_recv.at[at],
            device_id=in_plane((*onward, 0)),
            device_id_type=MESH,
        )

    def passed_on(offset):
        at = offset[0] * nx + offset[1]
        came_from = (y + ny - offset[0]) % ny * nx + (x + nx - offset[1]) % nx
        return pltpu.make_async_remote_copy(
            src_ref=key_slot(0, came_from),
            dst_ref=key_slot(1, came_from),
            send_sem=fwd_send.at[at],
            recv_sem=fwd_recv.at[at],
            device_id=sibling,
            device_id_type=MESH,
        )

    with jax.named_scope("gather_start"):
        for offset in key_direct[:2]:
            key_copy(offset).start()
        for k in query_direct[:2]:
            query_copy(k).start()
        for offset in key_direct[2:]:
            key_copy(offset).start()
        for k in query_direct[2:]:
            query_copy(k).start()
        passed_on((0, 0)).start()

    with jax.named_scope("gather_relay"):
        for offset in key_direct[2:] + key_direct[:2]:
            key_copy(offset).wait_recv()
            for further in key_relays:
                if key_via(further) == offset:
                    key_copy(further).start()
            passed_on(offset).start()
        for k in query_direct[:2]:
            query_copy(k).wait_recv()
            for further in query_relays:
                if query_via(further) == k:
                    query_copy(further).start()

    with jax.named_scope("key_pass_on"):
        for offset in key_relays[::-1]:
            key_copy(offset).wait_recv()
            passed_on(offset).start()

    with jax.named_scope("query_wait"):
        for k in query_direct[2:] + query_relays:
            query_copy(k).wait_recv()

    def scores_with(half):
        return lax.dot_general(
            queries[:, :width],
            keys[half * n_half : (half + 1) * n_half, :width],
            (((1,), (1,)), ((), ())),
            preferred_element_type=jnp.float32,
        ) * (1.0 / width**0.5)

    def down_log_sum_exp(values):
        peak = jnp.max(values, axis=0, keepdims=True)
        return peak + jnp.log(jnp.sum(jnp.exp(values - peak), axis=0, keepdims=True))

    with jax.named_scope("own_scores"):
        scores_own = scores_with(0)
        q_at = lax.broadcasted_iota(jnp.int32, (n_query, n_half), 0)
        k_at = lax.broadcasted_iota(jnp.int32, (n_query, n_half), 1)
        selfs = jnp.logical_and(k_at - q_at == rows * (chip - z), q_at // rows == z)
        masked_own = jnp.where(selfs, jnp.float32(-1e30), scores_own)
        lse_own = down_log_sum_exp(masked_own)

    with jax.named_scope("passed_wait"):
        for offset in [(0, 0)] + chips_away[::-1]:
            passed_on(offset).wait_recv()

    with jax.named_scope("scores"):
        scores_other = scores_with(1)
        masked = jnp.concatenate([masked_own, scores_other], axis=1)
        col_lse = jnp.concatenate([lse_own, down_log_sum_exp(scores_other)], axis=1)

    with jax.named_scope("positives"):
        same = lax.dot_general(
            queries[:, width:],
            keys[:, width:],
            (((1,), (1,)), ((), ())),
            preferred_element_type=jnp.float32,
        )
        same = jnp.where(same > 1.5, 1.0, 0.0)
        pos = jnp.concatenate(
            [jnp.where(selfs, 0.0, same[:, :n_half]), same[:, n_half:]], axis=1
        )

    with jax.named_scope("stats"):
        col_count = jnp.sum(pos, axis=0, keepdims=True)
        blocks = n_key // LANES
        for r in range(blocks):
            at = slice(r * LANES, (r + 1) * LANES)
            for turn in range(2):
                to = (r + turn * blocks // 2) % blocks
                col_mine[turn, 0, to : to + 1, :] = col_lse[:, at]
                col_mine[turn, 1, to : to + 1, :] = col_count[:, at]
        col_all[pl.ds(chip, 1)] = col_mine[0:1]

    def col_copy(offset):
        return pltpu.make_async_remote_copy(
            src_ref=col_mine.at[offset[2]],
            dst_ref=col_all.at[offset[2] * chips + chip],
            send_sem=col_sem.at[0],
            recv_sem=col_sem.at[1],
            device_id=in_plane(offset),
            device_id_type=MESH,
        )

    def row_copy(k):
        return pltpu.make_async_remote_copy(
            src_ref=row_mine,
            dst_ref=row_all.at[z],
            send_sem=row_sem.at[0],
            recv_sem=row_sem.at[1],
            device_id=in_ring(k),
            device_id_type=MESH,
        )

    with jax.named_scope("col_start"):
        for offset in others:
            col_copy(offset).start()

    with jax.named_scope("row_stats"):
        peak = jnp.max(masked, axis=1, keepdims=True)
        row_lse = peak + jnp.log(jnp.sum(jnp.exp(masked - peak), axis=1, keepdims=True))
        row_possum = jnp.sum(pos * masked, axis=1, keepdims=True)
        row_count = jnp.sum(pos, axis=1, keepdims=True)
        lane = lax.broadcasted_iota(jnp.int32, (n_query, LANES), 1)
        tall = jnp.where(lane == 0, row_lse, jnp.where(lane == 1, row_possum, row_count))
        row_mine[...] = jnp.transpose(tall)[:4]
        row_all[pl.ds(z, 1)] = row_mine[...][None]
        for k in ring:
            row_copy(k).start()

    with jax.named_scope("stats_wait"):
        wait_bytes(col_all.at[pl.ds(0, plane - 1)], col_sem.at[1])
        wait_bytes(row_all.at[pl.ds(0, nz - 1)], row_sem.at[1])

    def log_sum_exp(parts):
        peak = jnp.max(parts, axis=0)
        return peak + jnp.log(jnp.sum(jnp.exp(parts - peak[None]), axis=0))

    with jax.named_scope("weights"):
        key_lse = log_sum_exp(col_all[:, 0])
        key_inverse = 1.0 / jnp.sum(col_all[:, 1], axis=0)
        query_lse = log_sum_exp(row_all[:, 0:1])
        query_possum = jnp.sum(row_all[:, 1:2], axis=0)
        query_inverse = 1.0 / jnp.sum(row_all[:, 2:3], axis=0)
        tall_lse = jnp.transpose(jnp.broadcast_to(query_lse, (LANES, n_query)))[:, :1]
        tall_inverse = jnp.transpose(jnp.broadcast_to(query_inverse, (LANES, n_query)))[:, :1]
        flat_lse = jnp.concatenate([key_lse[r : r + 1] for r in range(n_key // LANES)], axis=1)
        flat_inverse = jnp.concatenate(
            [key_inverse[r : r + 1] for r in range(n_key // LANES)], axis=1
        )
        weight = (jnp.exp(masked - tall_lse) - pos * tall_inverse) * (1.0 / whole)
        mirrored = (jnp.exp(masked - flat_lse) - pos * flat_inverse) * (1.0 / whole)

    with jax.named_scope("gradient"):
        weight = weight.astype(jnp.bfloat16)
        mirrored = mirrored.astype(jnp.bfloat16)

    def part_copy(to):
        return pltpu.make_async_remote_copy(
            src_ref=part_mine.at[pl.ds(to * rows, rows)],
            dst_ref=part_all.at[z],
            send_sem=part_sem.at[0],
            recv_sem=part_sem.at[1],
            device_id=(y, to, x, c),
            device_id_type=MESH,
        )

    def loss_copy(offset):
        return pltpu.make_async_remote_copy(
            src_ref=loss_mine,
            dst_ref=loss_all.at[offset[2] * chips + chip],
            send_sem=loss_sem.at[0],
            recv_sem=loss_sem.at[1],
            device_id=in_plane(offset),
            device_id_type=MESH,
        )

    with jax.named_scope("reduce_start"):
        some = n_query // 2
        for first in range(0, n_query, some):
            last = first + some
            both = jnp.concatenate([weight[first:last], mirrored[first:last]], axis=0)
            terms = jnp.dot(both, keys[:, :width], preferred_element_type=jnp.float32)
            terms = (terms[:some] + terms[some:]) * (1.0 / width**0.5)
            part_mine[first:last] = terms.astype(jnp.bfloat16)
            for to in range(first // rows, last // rows):

                @pl.when(z != to)
                def _():
                    part_copy(to).start()

        part_all[pl.ds(z, 1)] = part_mine[pl.ds(pl.multiple_of(z * rows, rows), rows), :][None]

    with jax.named_scope("loss_start"):
        loss_mine[...] = query_lse - query_possum * query_inverse
        loss_all[pl.ds(chip, 1)] = loss_mine[...][None]
        for offset in others:
            loss_copy(offset).start()

    with jax.named_scope("gather_sent"):
        for k in ring:
            query_copy(k).wait_send()
        for offset in chips_away:
            key_copy(offset).wait_send()
        for offset in [(0, 0)] + chips_away:
            passed_on(offset).wait_send()

    with jax.named_scope("stats_sent"):
        wait_bytes(col_all.at[pl.ds(0, plane - 1)], col_sem.at[0])
        wait_bytes(row_all.at[pl.ds(0, nz - 1)], row_sem.at[0])

    with jax.named_scope("part_sent"):
        wait_bytes(part_all.at[pl.ds(0, nz - 1)], part_sem.at[0])

    with jax.named_scope("loss_sent"):
        wait_bytes(loss_all.at[pl.ds(0, plane - 1)], loss_sem.at[0])

    with jax.named_scope("loss_wait"):
        wait_bytes(loss_all.at[pl.ds(0, plane - 1)], loss_sem.at[1])
        total = jnp.sum(loss_all[...], axis=0)
        loss_ref[...] = jnp.broadcast_to(jnp.sum(total, axis=1, keepdims=True) * (1.0 / whole), (8, 128))

    with jax.named_scope("reduce_wait"):
        wait_bytes(part_all.at[pl.ds(0, nz - 1)], part_sem.at[1])
        grad_ref[...] = jnp.sum(part_all[...].astype(jnp.float32), axis=0).astype(jnp.bfloat16)


def on_device(embeddings, group_ids):
    ny, nz, nx, nc = (lax.axis_size(a) for a in ALL)
    rows, width = embeddings.shape
    chips = ny * nx
    plane = chips * nc
    n_query, n_key = nz * rows, plane * rows
    dma = pltpu.SemaphoreType.DMA
    loss, grad = pl.pallas_call(
        functools.partial(kernel, (ny, nz, nx, nc, rows, width)),
        out_shape=(
            pltpu.VMEM((8, 128), jnp.float32),
            pltpu.VMEM((rows, width), jnp.bfloat16),
        ),
        in_specs=[pl.BlockSpec(memory_space=pltpu.HBM)] * 2,
        out_specs=(
            pl.BlockSpec(memory_space=pltpu.VMEM),
            pl.BlockSpec(memory_space=pltpu.VMEM),
        ),
        scratch_shapes=[
            pltpu.VMEM((n_key, width + IDS), jnp.bfloat16),
            pltpu.VMEM((n_query, width + IDS), jnp.bfloat16),
            pltpu.SMEM((rows,), jnp.int32),
            pltpu.VMEM((2, 2, n_key // LANES, LANES), jnp.float32),
            pltpu.VMEM((plane, 2, n_key // LANES, LANES), jnp.float32),
            pltpu.VMEM((4, n_query), jnp.float32),
            pltpu.VMEM((nz, 4, n_query), jnp.float32),
            pltpu.VMEM((n_query, width), jnp.bfloat16),
            pltpu.VMEM((nz, rows, width), jnp.bfloat16),
            pltpu.VMEM((1, n_query), jnp.float32),
            pltpu.VMEM((plane, 1, n_query), jnp.float32),
            dma((2,)),
            dma((chips,)),
            dma((chips,)),
            dma((chips,)),
            dma((chips,)),
            dma((nz,)),
            dma((nz,)),
            dma((2,)),
            dma((2,)),
            dma((2,)),
            dma((2,)),
        ],
        compiler_params=pltpu.CompilerParams(
            collective_id=0, has_side_effects=True, vmem_limit_bytes=60 * 1024 * 1024
        ),
    )(embeddings, group_ids)

    def finish(loss_in, grad_in, loss_out, grad_out):
        loss_out[...] = loss_in[:1, :1]
        grad_out[...] = grad_in[...]

    loss, grad = pl.pallas_call(
        finish,
        out_shape=(
            jax.ShapeDtypeStruct((1, 1), jnp.float32),
            jax.ShapeDtypeStruct((rows, width), jnp.bfloat16),
        ),
        in_specs=[pl.BlockSpec(memory_space=pltpu.VMEM)] * 2,
        compiler_params=pltpu.CompilerParams(vmem_limit_bytes=1024 * 1024),
    )(loss, grad)
    return loss.reshape(()), grad


def solution(mesh):
    split = Mesh(mesh.devices.reshape(4, 8, 4, 2), ALL)
    return jax.shard_map(
        on_device,
        mesh=split,
        in_specs=(P(ALL, None), P(ALL)),
        out_specs=(P(), P(ALL, None)),
        check_vma=False,
    )
```

```python
import functools

import jax
import jax.numpy as jnp
from jax import lax
from jax.experimental import pallas as pl
from jax.experimental.pallas import tpu as pltpu
from jax.sharding import Mesh
from jax.sharding import PartitionSpec as P

MESH = pl.DeviceIdType.MESH
ALL = ("y", "z", "x", "c")
LANES = 128
IDS = 128
HALF = 32


def wait_bytes(ref, sem):
    pltpu.make_async_copy(ref, ref, sem).wait()


def kernel(
    sizes,
    emb_ref,
    ids_ref,
    loss_ref,
    grad_ref,
    keys,
    queries,
    ids_smem,
    col_mine,
    col_all,
    row_mine,
    row_all,
    part_mine,
    part_all,
    loss_mine,
    loss_all,
    in_sem,
    key_send,
    key_recv,
    fwd_send,
    fwd_recv,
    query_send,
    query_recv,
    col_sem,
    row_sem,
    part_sem,
    loss_sem,
):
    ny, nz, nx, nc, rows, width = sizes
    chips = ny * nx
    plane = chips * nc
    n_query, n_key, n_half = nz * rows, plane * rows, chips * rows
    whole = n_query * plane
    y, z, x, c = (lax.axis_index(a) for a in ALL)
    chip = y * nx + x
    sibling = (y, z, x, 1 - c)

    ring = sorted(range(1, nz), key=lambda k: -min(k, nz - k))
    others = [(dy, dx, dc) for dy in range(ny) for dx in range(nx) for dc in range(nc)][1:]
    others.sort(key=lambda o: -min(o[0], ny - o[0]) - min(o[1], nx - o[1]))
    chips_away = [(dy, dx) for dy, dx, dc in others if dc == 0]

    def in_ring(k):
        return (y, (z + k) % nz, x, c)

    def in_plane(offset):
        dy, dx, dc = offset
        return ((y + dy) % ny, z, (x + dx) % nx, c if dc == 0 else 1 - c)

    def key_slot(half, k):
        start = half * n_half + pl.multiple_of(k * rows, rows)
        return keys.at[pl.ds(start, rows)]

    def query_via(k):
        if min(k, nz - k) < 3:
            return 0
        return 2 if k <= nz // 2 else nz - 2

    def key_via(offset):
        dy, dx = offset
        if dy == 0 or dx == 0:
            return (0, 0)
        if min(dy, ny - dy) == min(dx, nx - dx):
            return (dy, 0) if dy == dx else (0, dx)
        return (dy, 0) if min(dy, ny - dy) == 2 else (0, dx)

    query_direct = [k for k in ring if not query_via(k)]
    query_relays = [k for k in ring if query_via(k)]
    key_direct = [o for o in chips_away if not any(key_via(o))]
    key_direct.sort(key=lambda o: 0 if 2 in o else 1 if 0 not in o else 2)
    key_relays = [o for o in chips_away if any(key_via(o))]

    def query_slot(k):
        return queries.at[pl.ds(pl.multiple_of(k * rows, rows), rows)]

    load = pltpu.make_async_copy(emb_ref, key_slot(0, chip).at[:, pl.ds(0, width)], in_sem.at[0])
    load.start()
    load_ids = pltpu.make_async_copy(ids_ref, ids_smem, in_sem.at[1])
    load_ids.start()

    with jax.named_scope("barrier"):
        barrier = pltpu.get_barrier_semaphore()

        for offset in key_direct:
            pl.semaphore_signal(
                barrier, inc=1, device_id=in_plane((*offset, 0)), device_id_type=MESH
            )
        for k in query_direct:
            pl.semaphore_signal(barrier, inc=1, device_id=in_ring(k), device_id_type=MESH)
        pl.semaphore_signal(barrier, inc=1, device_id=sibling, device_id_type=MESH)

        load_ids.wait()
        at_row = lax.broadcasted_iota(jnp.int32, (rows, IDS), 0)
        lane = lax.broadcasted_iota(jnp.int32, (rows, IDS), 1)
        ids = jnp.zeros((rows, IDS), jnp.int32)
        for r in range(rows):
            ids = jnp.where(at_row == r, ids_smem[r], ids)
        hot = jnp.logical_or(
            lane == lax.shift_right_logical(ids, 5), lane == HALF + jnp.bitwise_and(ids, HALF - 1)
        )
        key_slot(0, chip)[:, width:] = jnp.where(hot, 1.0, 0.0).astype(jnp.bfloat16)
        load.wait()
        query_slot(z)[...] = key_slot(0, chip)[...]
        pl.semaphore_wait(barrier, len(key_direct) + len(query_direct) + 1)

    def query_copy(k):
        via = query_via(k)
        source = (z + nz - via) % nz
        return pltpu.make_async_remote_copy(
            src_ref=query_slot(source) if via else key_slot(0, chip),
            dst_ref=query_slot(source),
            send_sem=query_send.at[k],
            recv_sem=query_recv.at[k],
            device_id=in_ring((k + nz - via) % nz),
            device_id_type=MESH,
        )

    def key_copy(offset):
        at = offset[0] * nx + offset[1]
        via = key_via(offset)
        source = (y + ny - via[0]) % ny * nx + (x + nx - via[1]) % nx
        onward = ((offset[0] + ny - via[0]) % ny, (offset[1] + nx - via[1]) % nx)
        return pltpu.make_async_remote_copy(
            src_ref=key_slot(0, source),
            dst_ref=key_slot(0, source),
            send_sem=key_send.at[at],
            recv_sem=key_recv.at[at],
            device_id=in_plane((*onward, 0)),
            device_id_type=MESH,
        )

    lines = sorted(range(ny), key=lambda dy: min(dy, ny - dy))

    def passed_on(dy):
        line = pl.multiple_of((y + ny - dy) % ny * nx * rows, nx * rows)
        return pltpu.make_async_remote_copy(
            src_ref=keys.at[pl.ds(line, nx * rows)],
            dst_ref=keys.at[pl.ds(n_half + line, nx * rows)],
            send_sem=fwd_send.at[dy],
            recv_sem=fwd_recv.at[dy],
            device_id=sibling,
            device_id_type=MESH,
        )

    with jax.named_scope("gather_start"):
        for k in query_direct:
            query_copy(k).start()
        for offset in key_direct:
            key_copy(offset).start()

    with jax.named_scope("gather_relay"):
        for offset in key_direct[2:] + key_direct[:2]:
            key_copy(offset).wait_recv()
            for further in key_relays:
                if key_via(further) == offset:
                    key_copy(further).start()
        passed_on(0).start()
        for k in query_direct[:2]:
            query_copy(k).wait_recv()
            for further in query_relays:
                if query_via(further) == k:
                    query_copy(further).start()

    with jax.named_scope("key_pass_on"):
        for dy in lines[1:]:
            for offset in key_relays[::-1]:
                if offset[0] == dy:
                    key_copy(offset).wait_recv()
            passed_on(dy).start()

    with jax.named_scope("query_wait"):
        for k in query_direct[2:] + query_relays:
            query_copy(k).wait_recv()

    def scores_with(half):
        return lax.dot_general(
            queries[:, :width],
            keys[half * n_half : (half + 1) * n_half, :width],
            (((1,), (1,)), ((), ())),
            preferred_element_type=jnp.float32,
        ) * (1.0 / width**0.5)

    def down_log_sum_exp(values):
        peak = jnp.max(values, axis=0, keepdims=True)
        return peak + jnp.log(jnp.sum(jnp.exp(values - peak), axis=0, keepdims=True))

    with jax.named_scope("own_scores"):
        scores_own = scores_with(0)
        q_at = lax.broadcasted_iota(jnp.int32, (n_query, n_half), 0)
        k_at = lax.broadcasted_iota(jnp.int32, (n_query, n_half), 1)
        selfs = jnp.logical_and(k_at - q_at == rows * (chip - z), q_at // rows == z)
        masked_own = jnp.where(selfs, jnp.float32(-1e30), scores_own)
        lse_own = down_log_sum_exp(masked_own)

    with jax.named_scope("passed_wait"):
        for dy in lines:
            passed_on(dy).wait_recv()

    with jax.named_scope("scores"):
        scores_other = scores_with(1)
        masked = jnp.concatenate([masked_own, scores_other], axis=1)
        col_lse = jnp.concatenate([lse_own, down_log_sum_exp(scores_other)], axis=1)

    with jax.named_scope("positives"):
        same = lax.dot_general(
            queries[:, width:],
            keys[:, width:],
            (((1,), (1,)), ((), ())),
            preferred_element_type=jnp.float32,
        )
        same = jnp.where(same > 1.5, 1.0, 0.0)
        pos = jnp.concatenate(
            [jnp.where(selfs, 0.0, same[:, :n_half]), same[:, n_half:]], axis=1
        )

    with jax.named_scope("stats"):
        col_count = jnp.sum(pos, axis=0, keepdims=True)
        blocks = n_key // LANES
        for r in range(blocks):
            at = slice(r * LANES, (r + 1) * LANES)
            for turn in range(2):
                to = (r + turn * blocks // 2) % blocks
                col_mine[turn, 0, to : to + 1, :] = col_lse[:, at]
                col_mine[turn, 1, to : to + 1, :] = col_count[:, at]
        col_all[pl.ds(chip, 1)] = col_mine[0:1]

    def col_copy(offset):
        return pltpu.make_async_remote_copy(
            src_ref=col_mine.at[offset[2]],
            dst_ref=col_all.at[offset[2] * chips + chip],
            send_sem=col_sem.at[0],
            recv_sem=col_sem.at[1],
            device_id=in_plane(offset),
            device_id_type=MESH,
        )

    def row_copy(k):
        return pltpu.make_async_remote_copy(
            src_ref=row_mine,
            dst_ref=row_all.at[z],
            send_sem=row_sem.at[0],
            recv_sem=row_sem.at[1],
            device_id=in_ring(k),
            device_id_type=MESH,
        )

    far = [o for o in others if min(o[0], ny - o[0]) + min(o[1], nx - o[1]) > 2]

    with jax.named_scope("col_start"):
        for offset in far:
            col_copy(offset).start()

    with jax.named_scope("row_stats"):
        row_peak = jnp.max(masked, axis=1, keepdims=True)
        row_exps = jnp.exp(masked - row_peak)
        row_lse = row_peak + jnp.log(jnp.sum(row_exps, axis=1, keepdims=True))
        row_possum = jnp.sum(pos * masked, axis=1, keepdims=True)
        row_count = jnp.sum(pos, axis=1, keepdims=True)
        lane = lax.broadcasted_iota(jnp.int32, (n_query, LANES), 1)
        tall = jnp.where(lane == 0, row_lse, jnp.where(lane == 1, row_possum, row_count))
        row_mine[...] = jnp.transpose(tall)[:4]
        for k in ring:
            row_copy(k).start()
        for offset in others:
            if offset not in far:
                col_copy(offset).start()
        row_all[pl.ds(z, 1)] = row_mine[...][None]

    with jax.named_scope("stats_wait"):
        wait_bytes(col_all.at[pl.ds(0, plane - 1)], col_sem.at[1])
        wait_bytes(row_all.at[pl.ds(0, nz - 1)], row_sem.at[1])

    def log_sum_exp(parts):
        peak = jnp.max(parts, axis=0)
        return peak + jnp.log(jnp.sum(jnp.exp(parts - peak[None]), axis=0))

    with jax.named_scope("weights"):
        key_lse = log_sum_exp(col_all[:, 0])
        key_inverse = 1.0 / jnp.sum(col_all[:, 1], axis=0)
        query_lse = log_sum_exp(row_all[:, 0:1])
        query_possum = jnp.sum(row_all[:, 1:2], axis=0)
        query_inverse = 1.0 / jnp.sum(row_all[:, 2:3], axis=0)
        tall_lse = jnp.transpose(jnp.broadcast_to(query_lse, (LANES, n_query)))[:, :1]
        tall_inverse = jnp.transpose(jnp.broadcast_to(query_inverse, (LANES, n_query)))[:, :1]
        flat_lse = jnp.concatenate([key_lse[r : r + 1] for r in range(n_key // LANES)], axis=1)
        flat_inverse = jnp.concatenate(
            [key_inverse[r : r + 1] for r in range(n_key // LANES)], axis=1
        )
        weight = (jnp.exp(masked - tall_lse) - pos * tall_inverse) * (1.0 / whole)
        mirrored = (jnp.exp(masked - flat_lse) - pos * flat_inverse) * (1.0 / whole)

    with jax.named_scope("gradient"):
        weight = weight.astype(jnp.bfloat16)
        mirrored = mirrored.astype(jnp.bfloat16)

    def part_copy(to):
        return pltpu.make_async_remote_copy(
            src_ref=part_mine.at[pl.ds(to * rows, rows)],
            dst_ref=part_all.at[z],
            send_sem=part_sem.at[0],
            recv_sem=part_sem.at[1],
            device_id=(y, to, x, c),
            device_id_type=MESH,
        )

    def loss_copy(offset):
        return pltpu.make_async_remote_copy(
            src_ref=loss_mine,
            dst_ref=loss_all.at[offset[2] * chips + chip],
            send_sem=loss_sem.at[0],
            recv_sem=loss_sem.at[1],
            device_id=in_plane(offset),
            device_id_type=MESH,
        )

    with jax.named_scope("reduce_start"):
        some = n_query // 2
        for first in range(0, n_query, some):
            last = first + some
            both = jnp.concatenate([weight[first:last], mirrored[first:last]], axis=0)
            terms = jnp.dot(both, keys[:, :width], preferred_element_type=jnp.float32)
            terms = (terms[:some] + terms[some:]) * (1.0 / width**0.5)
            part_mine[first:last] = terms.astype(jnp.bfloat16)
            for to in range(first // rows, last // rows):

                @pl.when(z != to)
                def _():
                    part_copy(to).start()

        part_all[pl.ds(z, 1)] = part_mine[pl.ds(pl.multiple_of(z * rows, rows), rows), :][None]

    with jax.named_scope("loss_start"):
        loss_mine[...] = query_lse - query_possum * query_inverse
        loss_all[pl.ds(chip, 1)] = loss_mine[...][None]
        for offset in others:
            loss_copy(offset).start()

    with jax.named_scope("gather_sent"):
        for k in ring:
            query_copy(k).wait_send()
        for offset in chips_away:
            key_copy(offset).wait_send()
        for dy in lines:
            passed_on(dy).wait_send()

    with jax.named_scope("stats_sent"):
        wait_bytes(col_all.at[pl.ds(0, plane - 1)], col_sem.at[0])
        wait_bytes(row_all.at[pl.ds(0, nz - 1)], row_sem.at[0])

    with jax.named_scope("part_sent"):
        wait_bytes(part_all.at[pl.ds(0, nz - 1)], part_sem.at[0])

    with jax.named_scope("loss_sent"):
        wait_bytes(loss_all.at[pl.ds(0, plane - 1)], loss_sem.at[0])

    with jax.named_scope("loss_wait"):
        wait_bytes(loss_all.at[pl.ds(0, plane - 1)], loss_sem.at[1])
        total = jnp.sum(loss_all[...], axis=0)
        loss_ref[...] = jnp.broadcast_to(jnp.sum(total, axis=1, keepdims=True) * (1.0 / whole), (8, 128))

    with jax.named_scope("reduce_wait"):
        wait_bytes(part_all.at[pl.ds(0, nz - 1)], part_sem.at[1])
        grad_ref[...] = jnp.sum(part_all[...].astype(jnp.float32), axis=0).astype(jnp.bfloat16)


def on_device(embeddings, group_ids):
    ny, nz, nx, nc = (lax.axis_size(a) for a in ALL)
    rows, width = embeddings.shape
    chips = ny * nx
    plane = chips * nc
    n_query, n_key = nz * rows, plane * rows
    dma = pltpu.SemaphoreType.DMA
    loss, grad = pl.pallas_call(
        functools.partial(kernel, (ny, nz, nx, nc, rows, width)),
        out_shape=(
            pltpu.VMEM((8, 128), jnp.float32),
            pltpu.VMEM((rows, width), jnp.bfloat16),
        ),
        in_specs=[pl.BlockSpec(memory_space=pltpu.HBM)] * 2,
        out_specs=(
            pl.BlockSpec(memory_space=pltpu.VMEM),
            pl.BlockSpec(memory_space=pltpu.VMEM),
        ),
        scratch_shapes=[
            pltpu.VMEM((n_key, width + IDS), jnp.bfloat16),
            pltpu.VMEM((n_query, width + IDS), jnp.bfloat16),
            pltpu.SMEM((rows,), jnp.int32),
            pltpu.VMEM((2, 2, n_key // LANES, LANES), jnp.float32),
            pltpu.VMEM((plane, 2, n_key // LANES, LANES), jnp.float32),
            pltpu.VMEM((4, n_query), jnp.float32),
            pltpu.VMEM((nz, 4, n_query), jnp.float32),
            pltpu.VMEM((n_query, width), jnp.bfloat16),
            pltpu.VMEM((nz, rows, width), jnp.bfloat16),
            pltpu.VMEM((1, n_query), jnp.float32),
            pltpu.VMEM((plane, 1, n_query), jnp.float32),
            dma((2,)),
            dma((chips,)),
            dma((chips,)),
            dma((chips,)),
            dma((chips,)),
            dma((nz,)),
            dma((nz,)),
            dma((2,)),
            dma((2,)),
            dma((2,)),
            dma((2,)),
        ],
        compiler_params=pltpu.CompilerParams(
            collective_id=0, has_side_effects=True, vmem_limit_bytes=60 * 1024 * 1024
        ),
    )(embeddings, group_ids)

    def finish(loss_in, grad_in, loss_out, grad_out):
        loss_out[...] = loss_in[:1, :1]
        grad_out[...] = grad_in[...]

    loss, grad = pl.pallas_call(
        finish,
        out_shape=(
            jax.ShapeDtypeStruct((1, 1), jnp.float32),
            jax.ShapeDtypeStruct((rows, width), jnp.bfloat16),
        ),
        in_specs=[pl.BlockSpec(memory_space=pltpu.VMEM)] * 2,
        compiler_params=pltpu.CompilerParams(vmem_limit_bytes=1024 * 1024),
    )(loss, grad)
    return loss.reshape(()), grad


def solution(mesh):
    split = Mesh(mesh.devices.reshape(4, 8, 4, 2), ALL)
    return jax.shard_map(
        on_device,
        mesh=split,
        in_specs=(P(ALL, None), P(ALL)),
        out_specs=(P(), P(ALL, None)),
        check_vma=False,
    )
```
